256 devices in a mesh: dp: 32 (over z_lo, x, core), group: 8 (over y, z_hi).
Axes of the slice: x: 4, y: 4, z: 8 (z_hi: 2, z_lo: 4; z = z_hi * 4 + z_lo), core: 2. Of those that a mesh axis runs over, the one named last changes fastest.
Arguments:
- cotangent: bfloat16 [32768, 2048], P(('dp', 'group')), may hold values from -6 to 6
- gate_weights: bfloat16 [32768, 8], P(('dp', 'group')), may hold values from 0.019897461 to 0.5
- expert_ids: int32 [32768, 8], P(('dp', 'group')), may hold values from 0 to 63, all different within a row; in each aligned block of 128 rows (0 to 127, 128 to 255, ...) at most 20 rows name the same one
- saved_hidden: bfloat16 [64, 5120, 768], P('dp', 'group'), may hold values from -6 to 6
- base_down: bfloat16 [64, 768, 2048], P('dp'), may hold values from -0.0029296875 to 0.0029296875
- factor_in: float32 [64, 64, 768], P('dp', 'group'), may hold values from -0.09375 to 0.09375
- factor_out: float32 [64, 64, 2048], P('dp', 'group'), may hold values from -0.09375 to 0.09375
- mean_in: float32 [64, 64, 768], P('dp', 'group'), may hold values from -0.625 to 0.625
- mean_out: float32 [64, 64, 2048], P('dp', 'group'), may hold values from -0.375 to 0.375
- square_in: float32 [64, 64, 768], P('dp', 'group'), may hold values from 2.260992e-05 to 0.00011442586
- square_out: float32 [64, 64, 2048], P('dp', 'group'), may hold values from 8.47872e-06 to 4.2909694e-05
- decode_hidden: bfloat16 [2, 64, 1024, 768], P(None, 'dp', 'group'), may hold values from -6 to 6
- decode_ids: int32 [2, 4096, 8], P(None, ('dp', 'group')), may hold values from 0 to 63, all different within a row; in each aligned block of 16 rows (0 to 15, 16 to 31, ..., all dimensions but the last counted through in order) at most 4 rows name the same one
- decode_gates: float32 [2, 4096, 8], P(None, ('dp', 'group')), may hold values from 0.02 to 0.5
- residual_in: bfloat16 [2, 4096, 2048], P(None, ('dp', 'group')), may hold values from -0.0625 to 0.0625
Outputs:
- hidden_grad: bfloat16 [64, 5120, 768], P('dp', 'group')
- adapted_in: float32 [64, 64, 768], P('dp', 'group')
- averaged_in: float32 [64, 64, 768], P('dp', 'group')
- squared_in: float32 [64, 64, 768], P('dp', 'group')
- adapted_out: float32 [64, 64, 2048], P('dp', 'group')
- averaged_out: float32 [64, 64, 2048], P('dp', 'group')
- squared_out: float32 [64, 64, 2048], P('dp', 'group')
- residual_out: bfloat16 [2, 4096, 2048], P(None, ('dp', 'group'))
The draws below stay inside these ranges and needn't reach their ends.
Inputs may be any that keep to these rules, and one draw needn't show every extreme that they name: `expert_ids`: each row names 8 different experts. In each aligned block of 128 rows (the rows of one device) no expert is named by more than 20 rows, and in some block one expert is named by exactly 20 rows. `decode_ids`: each row names 8 different experts. Taking both leading dimensions in order, in each aligned block of 16 rows no expert is named by more than 4 rows, and in some block one expert is named by exactly 4 rows.
All inputs are finite; a program needn't handle non-finite values.
Results may differ from the reference program's by a relative error of at most 0.022.
Values may be sent and summed in bfloat16 or wider, within the bound.
A program may use at most 128 MiB of HBM per device.

```python
import math
import jax
import jax.numpy as jnp
import numpy as np
from jax import lax

D = 2048
FF = 768
RANK = 64
TOP = 8
EXP_DEV = 2
STEPS = 2
TOK_DEV = 128
DEC_DEV = 16
EXPERTS = 64
CAP = 20
CAPD = 4
SLOTS = 5120
DSLOTS = 1024
TOKENS = 32768
DEC_ROWS = 4096
N_DP = 32
N_GROUP = 8


def levels(key, extent, shards, low, top_value):
    level, own = 1.0, jax.random.fold_in(key, 6)
    for position, parts in shards:
        steps = jnp.exp(jax.random.uniform(jax.random.fold_in(own, position), (parts,), jnp.float32, low / len(shards), top_value / len(shards)))
        level = level * jnp.repeat(steps, extent[position] // parts).reshape([-1 if axis == position else 1 for axis in range(len(extent))])
    return level


def deal_out(stream_key, own, number, rows, number_of, top, limit, skew):
    order = jax.random.permutation(stream_key, number_of)
    crowded, usual = portions_of(number_of, rows * top, limit, skew, True), portions_of(number_of, rows * top, limit, skew, False)
    places = jnp.arange(number_of)

    def named(tallies, rotation):
        used = int((tallies > 0).sum())
        fixed = max(1, used // 4)
        passed = fixed + (places - fixed + rotation * (used - fixed)) % max(1, number_of - fixed)
        return jnp.zeros((number_of,), jnp.int32).at[order[jnp.where(places < fixed, places, passed)]].set(jnp.asarray(tallies, jnp.int32))

    tallies = jnp.where(number % 4 == 0, named(crowded, number // 4), named(usual, number - number // 4 - 1))
    mixed = jax.random.permutation(jax.random.fold_in(own, 3), number_of)
    source_of, taker = mixed[0:number_of // 2 * 2:2], mixed[1:number_of // 2 * 2:2]
    slack = jnp.minimum(tallies[source_of] - 1, limit - tallies[taker]) // 2
    slack = jnp.where((source_of == order[0]) | (taker == order[0]) | (tallies[taker] == 0), 0, jnp.maximum(slack, 0))
    passed = jax.random.randint(jax.random.fold_in(own, 4), (number_of // 2,), 0, 1 << 20) % (slack + 1)
    tallies = tallies.at[source_of].add(-passed).at[taker].add(passed)
    labels = jnp.searchsorted(jnp.cumsum(tallies), jnp.arange(rows * top), side="right").astype(jnp.int32)
    table = labels.reshape(top, rows).T
    table = table[jax.random.permutation(jax.random.fold_in(own, 1), rows)]
    rotation = jax.random.randint(jax.random.fold_in(own, 2), (rows, 1), 0, top)
    return jnp.take_along_axis(table, (jnp.arange(top)[None, :] + rotation) % top, axis=1)


def portions_of(amount, total, limit, skew, full):
    loads = [(1 << 20) // math.isqrt(standing ** skew) + 1 for standing in range(1, amount + 1)]
    largest = limit if full else min(limit, max(-(-total // amount), total * loads[0] // sum(loads)))
    least = 1 if total - largest >= amount - 1 else 0
    counts, surplus = [largest] + [least] * (amount - 1), total - largest - least * (amount - 1)
    while surplus > 0:
        candidates = [i for i in range(1, amount) if counts[i] < largest] or [i for i in range(1, amount) if counts[i] < limit]
        mass, budget = sum([loads[i] for i in candidates]), surplus
        for i in candidates:
            extra = min(limit - counts[i], max(1, budget * loads[i] // mass), surplus)
            counts[i] = counts[i] + extra
            surplus = surplus - extra
    return np.array(counts)


def normal_values(rng, extent, scale, limit, shards=(), held_as=jnp.bfloat16):
    loudness = levels(rng, extent, shards, -0.22, 0.18) if shards else 1.0
    array = jax.random.normal(rng, extent, jnp.float32) * scale * loudness
    return jnp.minimum(jnp.maximum(array, -limit), limit).astype(held_as)


def setup_inputs(seed: int = 0) -> dict:
    key_list = jax.random.split(jax.random.key(seed), 16)
    cotangent = normal_values(key_list[0], (TOKENS, D), 1.0, 6.0, ((0, 256),))
    gate_weights = jnp.clip(jnp.exp(math.log(0.5) - 3.224016 * jax.random.uniform(key_list[1], (TOKENS, TOP), jnp.float32) ** levels(key_list[1], (TOKENS, TOP), ((0, 256),), -0.2, 0.2)), 0.019897461, 0.5).astype(jnp.bfloat16)
    expert_ids_keys = jax.random.split(jax.random.fold_in(key_list[2], 1), TOKENS // TOK_DEV)
    expert_ids_turns = jax.random.permutation(jax.random.fold_in(key_list[2], 3), TOKENS // TOK_DEV)
    expert_ids = jax.vmap(lambda own, number: deal_out(jax.random.fold_in(key_list[2], 2), own, number, TOK_DEV, EXPERTS, TOP, CAP, 2))(expert_ids_keys, expert_ids_turns).reshape((TOKENS, TOP))
    saved_hidden = normal_values(key_list[3], (EXPERTS, SLOTS, FF), 1.0, 6.0, ((0, 32), (1, 8)))
    base_down = normal_values(key_list[4], (EXPERTS, FF, D), 0.0002, 0.0029296875, ((0, 32),))
    factor_in = normal_values(key_list[5], (EXPERTS, RANK, FF), 0.006, 0.09375, ((0, 32), (1, 8)), jnp.float32)
    factor_out = normal_values(key_list[6], (EXPERTS, RANK, D), 0.006, 0.09375, ((0, 32), (1, 8)), jnp.float32)
    mean_in = normal_values(key_list[7], (EXPERTS, RANK, FF), (0.000118 * (D * TOK_DEV * TOP // (N_GROUP * EXP_DEV)) ** 0.5), 0.625, ((0, 32), (1, 8)), jnp.float32)
    mean_out = normal_values(key_list[8], (EXPERTS, RANK, D), (0.000118 * (FF * TOK_DEV * TOP // (N_GROUP * EXP_DEV)) ** 0.5), 0.375, ((0, 32), (1, 8)), jnp.float32)
    square_in = jnp.clip(jnp.exp(math.log(0.00011442586) - 1.6215383 * jax.random.uniform(key_list[9], (EXPERTS, RANK, FF), jnp.float32) ** levels(key_list[9], (EXPERTS, RANK, FF), ((0, 32), (1, 8)), -0.2, 0.2)), 2.2609920051763766e-05, 0.00011442586)
    square_out = jnp.clip(jnp.exp(math.log(4.2909694457193837e-05) - 1.6215383 * jax.random.uniform(key_list[10], (EXPERTS, RANK, D), jnp.float32) ** levels(key_list[10], (EXPERTS, RANK, D), ((0, 32), (1, 8)), -0.2, 0.2)), 8.478719792037737e-06, 4.2909694457193837e-05)
    decode_hidden = normal_values(key_list[11], (STEPS, EXPERTS, DSLOTS, FF), 1.0, 6.0, ((1, 32), (2, 8)))
    decode_ids_keys = jax.random.split(jax.random.fold_in(key_list[12], 1), STEPS * DEC_ROWS // DEC_DEV)
    decode_ids_turns = jax.random.permutation(jax.random.fold_in(key_list[12], 3), STEPS * DEC_ROWS // DEC_DEV)
    decode_ids = jax.vmap(lambda own, number: deal_out(jax.random.fold_in(key_list[12], 2), own, number, DEC_DEV, EXPERTS, TOP, CAPD, 2))(decode_ids_keys, decode_ids_turns).reshape((STEPS, DEC_ROWS, TOP))
    decode_gates = jnp.clip(jnp.exp(math.log(0.5) - 3.218876 * jax.random.uniform(key_list[13], (STEPS, DEC_ROWS, TOP), jnp.float32) ** levels(key_list[13], (STEPS, DEC_ROWS, TOP), ((1, 256),), -0.2, 0.2)), 0.02, 0.5)
    residual_in = normal_values(key_list[14], (STEPS, DEC_ROWS, D), 0.004, 0.0625, ((1, 256),))
    return {"cotangent": cotangent, "gate_weights": gate_weights, "expert_ids": expert_ids, "saved_hidden": saved_hidden, "base_down": base_down, "factor_in": factor_in, "factor_out": factor_out, "mean_in": mean_in, "mean_out": mean_out, "square_in": square_in, "square_out": square_out, "decode_hidden": decode_hidden, "decode_ids": decode_ids, "decode_gates": decode_gates, "residual_in": residual_in}


delta_scale = 0.5
learn_rate = 0.005
beta_first = 0.9
beta_second = 0.999
adam_count = 20.0
adam_eps = 1e-08

def block_ranks(flat_ids, expert_count):
    onehot = (flat_ids[..., None] == jnp.arange(expert_count, dtype=jnp.int32)).astype(jnp.int32)
    running = jnp.cumsum(onehot, axis=-2)
    return lax.optimization_barrier(jnp.sum(running * onehot, axis=-1)) - 1

def slot_tables(chosen, gates, block_rows, capacity):
    blocks = chosen.shape[0] // block_rows
    flat_ids = chosen.reshape(blocks, block_rows * TOP)
    slot_rank = block_ranks(flat_ids, EXPERTS)
    shard_id = jnp.arange(blocks, dtype=jnp.int32)[:, None]
    dp_place = shard_id // N_GROUP
    group_place = shard_id % N_GROUP
    slot_row = group_place * (N_DP * capacity) + dp_place * capacity + slot_rank
    expert_span = N_GROUP * N_DP * capacity
    target = (flat_ids * expert_span + slot_row).reshape(-1)
    token_of = jnp.arange(blocks * block_rows * TOP, dtype=jnp.int32) // TOP
    token_table = jnp.zeros((EXPERTS * expert_span,), jnp.int32).at[target].set(token_of)
    gate_table = jnp.zeros((EXPERTS * expert_span,), gates.dtype).at[target].set(gates.reshape(-1))
    return (token_table.reshape(EXPERTS, expert_span), gate_table.reshape(EXPERTS, expert_span))

def adam_update(parameter, moment_one, moment_two, gradient):
    first_new = beta_first * moment_one + (1.0 - beta_first) * gradient
    second_new = beta_second * moment_two + (1.0 - beta_second) * gradient * gradient
    fix_first = 1.0 - beta_first ** adam_count
    fix_second = 1.0 - beta_second ** adam_count
    update = first_new / fix_first / (jnp.sqrt(second_new / fix_second) + adam_eps)
    return (parameter - learn_rate * update, first_new, second_new)

def reference(cotangent, gate_weights, expert_ids, saved_hidden, base_down, factor_in, factor_out, mean_in, mean_out, square_in, square_out, decode_hidden, decode_ids, decode_gates, residual_in):
    token_table, gate_table = slot_tables(expert_ids, gate_weights, TOK_DEV, CAP)
    learner_in = factor_in.astype(jnp.bfloat16)
    learner_out = factor_out.astype(jnp.bfloat16)

    def learner_expert(operands):
        hidden, token_rows, gate_rows, weight, delta_in, delta_out = operands
        picked = cotangent[token_rows].astype(jnp.float32)
        slot_cot = (gate_rows.astype(jnp.float32)[:, None] * picked).astype(jnp.bfloat16)
        low_in = jnp.dot(hidden, delta_in.T, preferred_element_type=jnp.float32).astype(jnp.bfloat16)
        low_out = jnp.dot(slot_cot, delta_out.T, preferred_element_type=jnp.float32).astype(jnp.bfloat16)
        base_part = jnp.dot(slot_cot, weight.T, preferred_element_type=jnp.float32)
        side_part = jnp.dot(low_out, delta_in, preferred_element_type=jnp.float32)
        hidden_cot = (base_part + delta_scale * side_part).astype(jnp.bfloat16)
        grad_in = delta_scale / N_GROUP * jnp.dot(low_out.T, hidden, preferred_element_type=jnp.float32)
        grad_out = delta_scale / N_GROUP * jnp.dot(low_in.T, slot_cot, preferred_element_type=jnp.float32)
        return (hidden_cot, grad_in, grad_out)
    hidden_grad, grad_in, grad_out = lax.map(learner_expert, (saved_hidden, token_table, gate_table, base_down, learner_in, learner_out))
    adapted_in, averaged_in, squared_in = adam_update(factor_in, mean_in, square_in, grad_in)
    adapted_out, averaged_out, squared_out = adam_update(factor_out, mean_out, square_out, grad_out)
    rollout_in = adapted_in.astype(jnp.bfloat16)
    rollout_out = adapted_out.astype(jnp.bfloat16)
    results = []
    for decode_step in range(STEPS):
        token_rows, gate_rows = slot_tables(decode_ids[decode_step], decode_gates[decode_step], DEC_DEV, CAPD)

        def expert_add(running_sum, operands):
            hidden, token_list, gate_list, weight, delta_in, delta_out = operands
            low_part = jnp.dot(hidden, delta_in.T, preferred_element_type=jnp.float32).astype(jnp.bfloat16)
            base_part = jnp.dot(hidden, weight, preferred_element_type=jnp.float32)
            side_part = jnp.dot(low_part, delta_out, preferred_element_type=jnp.float32)
            expert_out = (base_part + delta_scale * side_part).astype(jnp.bfloat16)
            return (running_sum.at[token_list].add(gate_list[:, None] * expert_out.astype(jnp.float32)), None)
        start_sum = residual_in[decode_step].astype(jnp.float32)
        final_sum, unused = lax.scan(expert_add, start_sum, (decode_hidden[decode_step], token_rows, gate_rows, base_down, rollout_in, rollout_out))
        results.append(final_sum.astype(jnp.bfloat16))
    residual_out = jnp.stack(results)
    return (hidden_grad, adapted_in, averaged_in, squared_in, adapted_out, averaged_out, squared_out, residual_out)
```

```python
import functools

import jax
import jax.numpy as jnp
from jax import lax
from jax.experimental import pallas as pl
from jax.experimental.pallas import tpu as pltpu
from jax.sharding import PartitionSpec as P

delta_scale = 0.5
learn_rate = 0.005
beta_first = 0.9
beta_second = 0.999
adam_count = 20.0
adam_eps = 1e-08

BF = jnp.bfloat16
F32 = jnp.float32
MESH = pl.DeviceIdType.MESH

NZ, NX, NC = 4, 4, 2
NQ = NX * NC
NY, NH = 4, 2
D, FF, CAP, CAPD = 2048, 768, 20, 4
TOK, DEC = 128, 32
NCH = 4
CW = D // NCH
SB = NZ * CAP
DB = NZ * 2 * CAPD
PIECES = ((0, 512), (512, 512), (1024, 512), (1536, 1280))
W = D + FF


def nt(a, b):
    return lax.dot_general(a, b, (((1,), (1,)), ((), ())), preferred_element_type=F32)


def tn(a, b):
    return lax.dot_general(a, b, (((0,), (0,)), ((), ())), preferred_element_type=F32)


def mm(a, b):
    return jnp.dot(a, b, preferred_element_type=F32)


def iota(shape, axis):
    return lax.broadcasted_iota(jnp.int32, shape, axis)


def adam_update(parameter, moment_one, moment_two, gradient):
    first_new = beta_first * moment_one + (1.0 - beta_first) * gradient
    second_new = beta_second * moment_two + (1.0 - beta_second) * gradient * gradient
    fix_first = 1.0 - beta_first**adam_count
    fix_second = 1.0 - beta_second**adam_count
    update = first_new / fix_first / (jnp.sqrt(second_new / fix_second) + adam_eps)
    return (parameter - learn_rate * update, first_new, second_new)


def kernel(
    ids_ref, gates_ref, dids_ref, dgates_ref, fin_ref, fout_ref,
    cot_hbm, saved_hbm, base_hbm, min_hbm, mout_hbm, sin_hbm, sout_hbm, dh_hbm, res_hbm,
    hg_hbm, ain_ref, vin_ref, qin_ref, aout_ref, vout_ref, qout_ref, rout_ref,
    xa, lms, lmr, dms, dmr, fg, pmat, lr, lg, ob, inc,
    saved, base, mi, mo, si, so, dh, res,
    perm, savedp, lit, lo, tg, ry, ss, sz, rz, rg,
    hgacc, hgp, hgn, dperm, dhp, dbase, amat, drs, pd, rd, pz, rzd,
    in_sem, out_sem, zt_s, zt_r, lm_s, lm_r, dm_s, dm_r, fz_s, fz_r, fy_s, fy_r,
    x_s, x_r, ry_s, ry_r, rz_s, rz_r, az_s, az_r, ay_s, ay_r, dx_s, dx_r, dz_s, dz_r,
):
    dp = lax.axis_index("dp")
    grp = lax.axis_index("group")
    z = dp // NQ
    q = dp % NQ
    x = q // NC
    c = q % NC
    y = grp // NH
    h = grp % NH

    def zdev(z2):
        return (z2 * NQ + q, grp)

    def qdev(q2):
        return (z * NQ + q2, grp)

    def ydev(y2):
        return (dp, y2 * NH + h)

    hdev = (dp, y * NH + (1 - h))
    zpeers = [(z + k) % NZ for k in (1, 2, 3)]
    ypeers = [(y + k) % NY for k in (2, 1, 3)]
    qpeers = [
        ((x + dx) % NX) * NC + (c + dc) % NC
        for dx, dc in ((2, 0), (2, 1), (1, 0), (3, 1), (1, 1), (3, 0), (0, 1))
    ]
    sends = []

    def push(src, dst, ssem, rsem, dev):
        cp = pltpu.make_async_remote_copy(
            src_ref=src, dst_ref=dst, send_sem=ssem, recv_sem=rsem, device_id=dev, device_id_type=MESH
        )
        cp.start()
        sends.append(cp)

    def arrived(dst, ssem, rsem, dev):
        pltpu.make_async_remote_copy(
            src_ref=dst, dst_ref=dst, send_sem=ssem, recv_sem=rsem, device_id=dev, device_id_type=MESH
        ).wait_recv()

    loads = {}

    def load(name, k, src, dst):
        cp = pltpu.make_async_copy(src, dst, in_sem.at[k])
        cp.start()
        loads[name] = cp

    own_rows = pl.ds(pl.multiple_of(z * TOK, TOK), TOK)
    for ch in range(NCH):
        load(("cot", ch), ch, cot_hbm.at[:, pl.ds(ch * CW, CW)], xa.at[ch, own_rows])
    load("saved", 4, saved_hbm, saved)
    load("base", 5, base_hbm, base)
    load("dh", 6, dh_hbm, dh)
    load("mi", 7, min_hbm, mi)
    load("mo", 8, mout_hbm, mo)
    load("si", 9, sin_hbm, si)
    load("so", 10, sout_hbm, so)
    load("res", 11, res_hbm, res)

    barrier = pltpu.get_barrier_semaphore()
    for z2 in zpeers:
        pl.semaphore_signal(barrier, inc=1, device_id=zdev(z2), device_id_type=MESH)
    for q2 in qpeers:
        pl.semaphore_signal(barrier, inc=1, device_id=qdev(q2), device_id_type=MESH)
    for y2 in ypeers:
        pl.semaphore_signal(barrier, inc=1, device_id=ydev(y2), device_id_type=MESH)
    pl.semaphore_signal(barrier, inc=1, device_id=hdev, device_id_type=MESH)

    own = pl.ds(grp, 1)
    fg[own, :, 0:D] = fout_ref[...].astype(BF)[None]
    fg[own, :, D:W] = fin_ref[...].astype(BF)[None]

    lane = iota((TOK, 128), 1)
    count = jnp.zeros((TOK, 128), F32)
    gate = jnp.zeros((TOK, 128), F32)
    ids = ids_ref[...]
    gw = gates_ref[...].astype(F32)
    for k in range(8):
        hit = ids[:, k : k + 1] == lane
        count = count + jnp.where(hit, 1.0, 0.0)
        gate = gate + jnp.where(hit, gw[:, k : k + 1], 0.0)
    rows, cols = iota((TOK, TOK), 0), iota((TOK, TOK), 1)
    before = jnp.where(rows < cols, 1.0, 0.0).astype(BF)
    eye = jnp.where(rows == cols, 1.0, 0.0).astype(BF)
    cb = count.astype(BF)
    rank_t = tn(cb, before)
    count_t = tn(cb, eye)
    gate_t = tn(gate.astype(BF), eye)
    row_t = jnp.where(count_t > 0.5, rank_t + (CAP * z).astype(F32), -1.0).astype(BF)
    gate_t = gate_t.astype(BF)
    for z2 in range(NZ):
        lms[z2, 0:16] = row_t[16 * z2 : 16 * z2 + 16]
        lms[z2, 16:32] = gate_t[16 * z2 : 16 * z2 + 16]

    lane = iota((DEC, 128), 1)
    count = jnp.zeros((DEC, 128), F32)
    gate = jnp.zeros((DEC, 128), F32)
    ids = dids_ref[...]
    gw = dgates_ref[...]
    for k in range(8):
        hit = ids[:, k : k + 1] == lane
        count = count + jnp.where(hit, 1.0, 0.0)
        gate = gate + jnp.where(hit, gw[:, k : k + 1], 0.0)
    rows, cols = iota((DEC, DEC), 0), iota((DEC, DEC), 1)
    before = jnp.where((cols < rows) & ((cols >> 4) == (rows >> 4)), 1.0, 0.0).astype(BF)
    rank = mm(before, count.astype(BF))
    high = gate.astype(BF)
    dms[0:32] = jnp.where(count > 0.5, rank, -1.0).astype(BF)
    dms[32:64] = high
    dms[64:96] = (gate - high.astype(F32)).astype(BF)

    pl.semaphore_wait(barrier, 14)

    push(fg.at[own], fg.at[own], fz_s.at[0], fz_r.at[0], hdev)
    for k, z2 in enumerate(zpeers):
        push(lms.at[z2], lmr.at[z], lm_s.at[k], lm_r.at[z], zdev(z2))

    def send_tokens(ch):
        loads[("cot", ch)].wait()
        for k, z2 in enumerate(zpeers):
            push(xa.at[ch, own_rows], xa.at[ch, own_rows], zt_s.at[ch, k], zt_r.at[ch, z], zdev(z2))

    send_tokens(0)
    send_tokens(1)
    for k, z2 in enumerate(zpeers):
        push(dms, dmr.at[z], dm_s.at[k], dm_r.at[z], zdev(z2))
    lmr[pl.ds(z, 1)] = lms[pl.ds(z, 1)]
    dmr[pl.ds(z, 1)] = dms[...][None]

    pair = pl.ds(pl.multiple_of(y * NH, NH), NH)
    other = pl.ds(y * NH + (1 - h), 1)
    arrived(fg.at[other], fz_s.at[0], fz_r.at[0], hdev)
    for k, y2 in enumerate(ypeers):
        push(fg.at[pair], fg.at[pair], fy_s.at[k], fy_r.at[y], ydev(y2))

    for z2 in zpeers:
        arrived(lmr.at[z2], lm_s.at[0], lm_r.at[z2], zdev(z2))
    for z2 in range(NZ):
        lr[:, z2 * TOK : (z2 + 1) * TOK] = lmr[z2, 0:16].astype(F32)
        lg[:, z2 * TOK : (z2 + 1) * TOK] = lmr[z2, 16:32].astype(F32)
    slot = iota((SB, NZ * TOK), 0).astype(F32)

    def build_p(e, carry):
        row = lr[pl.ds(e, 1), :]
        val = lg[pl.ds(e, 1), :]
        pmat[e] = jnp.where(slot == row, val, 0.0).astype(BF)
        return carry

    lax.fori_loop(0, 2 * NQ, build_p, 0)

    def expand(ch, q2):
        w = pmat[pl.ds(q2 * 2, 2)].reshape(2 * SB, NZ * TOK)
        return mm(w, xa[ch]).astype(BF).reshape(2, SB, CW)

    def build_send(ch):
        for z2 in zpeers:
            dst = xa.at[ch, pl.ds(pl.multiple_of(z2 * TOK, TOK), TOK)]
            arrived(dst, zt_s.at[ch, 0], zt_r.at[ch, z2], zdev(z2))
        if ch + 2 < NCH:
            send_tokens(ch + 2)
        for k, q2 in enumerate(qpeers):
            ob[ch, k] = expand(ch, q2)
            push(ob.at[ch, k], inc.at[ch, :, q], x_s.at[ch, k], x_r.at[ch, q], qdev(q2))
        inc[ch, :, pl.ds(q, 1)] = expand(ch, q)[:, None]

    build_send(0)

    def permutation(n, source):
        return jnp.where(iota((n, n), 1) == source, 1.0, 0.0).astype(BF)

    p_id = iota((NQ * SB, NQ * SB), 0)
    blk = (p_id * 3277) >> 16
    off = p_id - blk * CAP
    perm[0] = permutation(NQ * SB, (blk & 3) * (NQ * CAP) + (blk >> 2) * CAP + off)
    perm[1] = permutation(NQ * SB, (blk & 7) * SB + (blk >> 3) * CAP + off)
    loads["saved"].wait()

    def permute_saved(e, carry):
        savedp[e] = mm(perm[0], saved[e]).astype(BF)
        return carry

    lax.fori_loop(0, 2, permute_saved, 0)

    for y2 in ypeers:
        blocks = pl.ds(pl.multiple_of(y2 * NH, NH), NH)
        arrived(fg.at[blocks], fy_s.at[0], fy_r.at[y2], ydev(y2))

    def lane_mask(n, e):
        return ((iota((n, 128), 1) >> 3) & 1) == e

    def low_in(e, carry):
        low = nt(savedp[e], fg[:, :, D:W].reshape(128, FF))
        low = jnp.where(lane_mask(NQ * SB, e), low, 0.0)
        lit[e] = low.T.astype(BF)
        lo[e] = jnp.zeros((NQ * SB, 128), F32)
        return carry

    lax.fori_loop(0, 2, low_in, 0)

    build_send(1)

    def consume(ch):
        for q2 in qpeers:
            arrived(inc.at[ch, :, q2], x_s.at[ch, 0], x_r.at[ch, q2], qdev(q2))
        cc = pl.ds(ch * CW, CW)
        weights = fg[:, :, cc].reshape(128, CW)

        def one(e, acc):
            rows = inc[ch, e].reshape(NQ * SB, CW)
            lo[e] += nt(rows, weights)
            return acc + mm(lit[e], rows)

        term = lax.fori_loop(0, 2, one, jnp.zeros((128, CW), F32))
        tg[:, :, cc] = term.astype(BF).reshape(8, 16, CW)

    def cols_of(p):
        return pl.ds(PIECES[p][0], PIECES[p][1])

    def rs_start(p):
        cc = cols_of(p)
        for k, y2 in enumerate(ypeers):
            src = tg.at[pl.ds(pl.multiple_of(y2 * NH, NH), NH), :, cc]
            push(src, ry.at[y, :, :, cc], ry_s.at[p, k], ry_r.at[p, y], ydev(y2))
        ry[pl.ds(y, 1), :, :, cc] = tg[pair, :, cc][None]

    def rs_mid(p):
        cc = cols_of(p)
        for y2 in ypeers:
            arrived(ry.at[y2, :, :, cc], ry_s.at[p, 0], ry_r.at[p, y2], ydev(y2))
        total = ry[0, :, :, cc].astype(F32)
        for y2 in range(1, NY):
            total = total + ry[y2, :, :, cc].astype(F32)
        ss[:, :, cc] = total
        sz[:, cc] = ss[1 - h, :, cc].astype(BF)
        push(sz.at[:, cc], rz.at[:, cc], rz_s.at[p], rz_r.at[p], hdev)

    def rs_fin(p):
        cc = cols_of(p)
        arrived(rz.at[:, cc], rz_s.at[p], rz_r.at[p], hdev)
        share = delta_scale / (NY * NH)

        def grad(start, width):
            at = pl.ds(start, width)
            return share * (ss[h, :, at] + rz[:, at].astype(F32))

        start = PIECES[p][0]
        at = pl.ds(start, CW)
        new, first, second = adam_update(fout_ref[:, at], mo[:, at], so[:, at], grad(start, CW))
        aout_ref[:, at], vout_ref[:, at], qout_ref[:, at] = new, first, second
        rg[own, :, at] = new.astype(BF)[None]
        if p == NCH - 1:
            new, first, second = adam_update(fin_ref[...], mi[...], si[...], grad(D, FF))
            ain_ref[...], vin_ref[...], qin_ref[...] = new, first, second
            rg[own, :, D:W] = new.astype(BF)[None]
        push(rg.at[own, :, cc], rg.at[own, :, cc], az_s.at[p], az_r.at[p], hdev)

    def ag_mid(p):
        cc = cols_of(p)
        arrived(rg.at[other, :, cc], az_s.at[p], az_r.at[p], hdev)
        for k, y2 in enumerate(ypeers):
            push(rg.at[pair, :, cc], rg.at[pair, :, cc], ay_s.at[p, k], ay_r.at[p, y], ydev(y2))

    def ag_fin(p):
        cc = cols_of(p)
        for y2 in ypeers:
            blocks = pl.ds(pl.multiple_of(y2 * NH, NH), NH)
            arrived(rg.at[blocks, :, cc], ay_s.at[p, 0], ay_r.at[p, y2], ydev(y2))

    n = iota((512, 512), 0)
    source = ((n >> 2) & 1) * 256 + (n >> 8) * 128 + ((n >> 3) & 3) * 32 + ((n >> 5) & 7) * 4 + (n & 3)
    dperm[...] = permutation(512, source)
    loads["dh"].wait()
    dhp[...] = mm(dperm[...], dh[...]).astype(BF).reshape(2, 256, FF)
    loads["base"].wait()

    def base_product(k, carry):
        e, ch = k // NCH, k % NCH
        at = pl.ds(pl.multiple_of(ch * CW, CW), CW)
        dbase[e, :, at] = mm(dhp[e], base[e, :, at])
        return carry

    lax.fori_loop(0, 2 * NCH, base_product, 0)

    consume(0)
    rs_start(0)
    build_send(2)

    for z2 in zpeers:
        arrived(dmr.at[z2], dm_s.at[0], dm_r.at[z2], zdev(z2))
    for z2 in range(NZ):
        for k in range(3):
            drs[k, z2 * DEC : (z2 + 1) * DEC] = dmr[z2, k * DEC : (k + 1) * DEC]
    j = iota((128, 512), 1)
    spread = jnp.where(iota((128, 512), 0) == z * 16 + (j >> 5), 1.0, 0.0).astype(BF)
    i = iota((128, 512), 0)
    ok = (mm(drs[0], spread) == (j & 3).astype(F32)) & ((i >> 5) == ((j >> 3) & 3)) & (((i >> 4) & 1) == ((j >> 2) & 1))
    amat[0] = jnp.where(ok, mm(drs[1], spread), 0.0).astype(BF)
    amat[1] = jnp.where(ok, mm(drs[2], spread), 0.0).astype(BF)

    for name in ("mi", "mo", "si", "so", "res"):
        loads[name].wait()

    consume(1)
    rs_start(1)
    rs_mid(0)
    build_send(3)
    consume(2)
    rs_start(2)
    rs_mid(1)
    rs_fin(0)
    consume(3)

    def term_in(e, acc):
        low = jnp.where(lane_mask(NQ * SB, e), lo[e], 0.0)
        lo[e] = low
        return acc + mm(low.T.astype(BF), savedp[e])

    term = lax.fori_loop(0, 2, term_in, jnp.zeros((128, FF), F32))
    tg[:, :, D:W] = term.astype(BF).reshape(8, 16, FF)
    rs_start(3)
    rs_mid(2)
    rs_fin(1)
    ag_mid(0)

    def hidden(e):
        hgacc[...] = delta_scale * mm(lo[e].astype(BF), fg[:, :, D:W].reshape(128, FF))

        def part(ch, carry):
            at = pl.ds(pl.multiple_of(ch * CW, CW), CW)
            hgacc[...] += nt(inc[ch, e].reshape(NQ * SB, CW), base[e, :, at])
            return carry

        lax.fori_loop(0, NCH, part, 0)
        hgp[...] = hgacc[...].astype(BF)
        hgn[e] = mm(perm[1], hgp[...]).astype(BF)
        cp = pltpu.make_async_copy(hgn.at[e], hg_hbm.at[e], out_sem.at[e])
        cp.start()
        return cp

    out0 = hidden(0)
    rs_mid(3)
    rs_fin(2)
    ag_mid(1)
    rs_fin(3)
    ag_mid(2)
    out1 = hidden(1)
    ag_mid(3)
    ag_fin(0)
    ag_fin(1)
    ag_fin(2)
    ag_fin(3)

    low_d = []
    for e in range(2):
        low = nt(dhp[e], rg[:, :, D:W].reshape(128, FF))
        low_d.append(jnp.where(lane_mask(256, e), low, 0.0).astype(BF))
    for ch in range(NCH):
        at = pl.ds(ch * CW, CW)
        weights = rg[:, :, at].reshape(128, CW)
        for e in range(2):
            made = dbase[e, :, at] + delta_scale * mm(low_d[e], weights)
            pd[ch, :, e] = made.astype(BF).reshape(NQ, DB, CW)
        for k, q2 in enumerate(qpeers):
            push(pd.at[ch, q2], rd.at[ch, q], dx_s.at[ch, k], dx_r.at[ch, q], qdev(q2))
        rd[ch, pl.ds(q, 1)] = pd[ch, pl.ds(q, 1)]
    for ch in range(NCH):
        for q2 in qpeers:
            arrived(rd.at[ch, q2], dx_s.at[ch, 0], dx_r.at[ch, q2], qdev(q2))
        rows = rd[ch].reshape(512, CW)
        part = mm(amat[0], rows) + mm(amat[1], rows)
        pz[ch] = part.astype(BF).reshape(NZ, DEC, CW)
        for k, z2 in enumerate(zpeers):
            push(pz.at[ch, z2], rzd.at[ch, z], dz_s.at[ch, k], dz_r.at[ch, z], zdev(z2))
        rzd[ch, pl.ds(z, 1)] = pz[ch, pl.ds(z, 1)]
    for ch in range(NCH):
        at = pl.ds(ch * CW, CW)
        for z2 in zpeers:
            arrived(rzd.at[ch, z2], dz_s.at[ch, 0], dz_r.at[ch, z2], zdev(z2))
        total = res[:, at].astype(F32)
        for z2 in range(NZ):
            total = total + rzd[ch, z2].astype(F32)
        rout_ref[:, at] = total.astype(BF)

    out0.wait()
    out1.wait()
    for cp in sends:
        cp.wait_send()


def on_device(
    cotangent, gate_weights, expert_ids, saved_hidden, base_down, factor_in, factor_out,
    mean_in, mean_out, square_in, square_out, decode_hidden, decode_ids, decode_gates, residual_in,
):
    flat = lambda a: a.reshape(16, a.shape[-1])
    vm = pl.BlockSpec(memory_space=pltpu.VMEM)
    hbm = pl.BlockSpec(memory_space=pl.ANY)
    sds = jax.ShapeDtypeStruct
    V = pltpu.VMEM
    S = pltpu.SemaphoreType.DMA
    n = NQ * SB
    scratch = [
        V((NCH, NZ * TOK, CW), BF),
        V((NZ, 32, TOK), BF), V((NZ, 32, TOK), BF), V((96, 128), BF), V((NZ, 96, 128), BF),
        V((8, 16, W), BF),
        V((2 * NQ, SB, NZ * TOK), BF), V((16, NZ * TOK), F32), V((16, NZ * TOK), F32),
        V((NCH, 7, 2, SB, CW), BF), V((NCH, 2, NQ, SB, CW), BF),
        V((2, n, FF), BF), V((2, FF, D), BF),
        V((16, FF), F32), V((16, D), F32), V((16, FF), F32), V((16, D), F32),
        V((512, FF), BF), V((DEC, D), BF),
        V((2, n, n), BF), V((2, n, FF), BF), V((2, 128, n), BF), V((2, n, 128), F32),
        V((8, 16, W), BF), V((NY, NH, 16, W), BF), V((NH, 16, W), F32),
        V((16, W), BF), V((16, W), BF), V((8, 16, W), BF),
        V((n, FF), F32), V((n, FF), BF), V((2, n, FF), BF),
        V((512, 512), BF), V((2, 256, FF), BF), V((2, 256, D), F32),
        V((2, 128, 512), BF), V((3, 128, 128), BF),
        V((NCH, NQ, 2, DB, CW), BF), V((NCH, NQ, 2, DB, CW), BF),
        V((NCH, NZ, DEC, CW), BF), V((NCH, NZ, DEC, CW), BF),
        S((12,)), S((2,)), S((NCH, 3)), S((NCH, NZ)), S((3,)), S((NZ,)), S((3,)), S((NZ,)),
        S((1,)), S((1,)), S((3,)), S((NY,)),
        S((NCH, 7)), S((NCH, NQ)), S((NCH, 3)), S((NCH, NY)), S((NCH,)), S((NCH,)),
        S((NCH,)), S((NCH,)), S((NCH, 3)), S((NCH, NY)),
        S((NCH, 7)), S((NCH, NQ)), S((NCH, 3)), S((NCH, NZ)),
    ]
    outs = pl.pallas_call(
        kernel,
        out_shape=(
            sds((2, n, FF), BF),
            sds((16, FF), F32), sds((16, FF), F32), sds((16, FF), F32),
            sds((16, D), F32), sds((16, D), F32), sds((16, D), F32),
            sds((DEC, D), BF),
        ),
        in_specs=[vm] * 6 + [hbm] * 9,
        out_specs=(hbm,) + (vm,) * 7,
        scratch_shapes=scratch,
        compiler_params=pltpu.CompilerParams(
            collective_id=0, has_side_effects=True, vmem_limit_bytes=60 * 1024 * 1024
        ),
    )(
        expert_ids, gate_weights, decode_ids.reshape(DEC, 8), decode_gates.reshape(DEC, 8),
        flat(factor_in), flat(factor_out),
        cotangent, saved_hidden, base_down, flat(mean_in), flat(mean_out), flat(square_in), flat(square_out),
        decode_hidden.reshape(512, FF), residual_in.reshape(DEC, D),
    )
    hg, ain, vin, qin, aout, vout, qout, rout = outs
    wide = lambda a: a.reshape(2, 8, a.shape[-1])
    return (
        hg, wide(ain), wide(vin), wide(qin), wide(aout), wide(vout), wide(qout),
        rout.reshape(2, DEC // 2, D),
    )


def solution(mesh):
    in_specs = (
        P(("dp", "group"), None),
        P(("dp", "group"), None),
        P(("dp", "group"), None),
        P("dp", "group", None),
        P("dp", None, None),
        P("dp", "group", None),
        P("dp", "group", None),
        P("dp", "group", None),
        P("dp", "group", None),
        P("dp", "group", None),
        P("dp", "group", None),
        P(None, "dp", "group", None),
        P(None, ("dp", "group"), None),
        P(None, ("dp", "group"), None),
        P(None, ("dp", "group"), None),
    )
    out_specs = (
        P("dp", "group", None),
        P("dp", "group", None),
        P("dp", "group", None),
        P("dp", "group", None),
        P("dp", "group", None),
        P("dp", "group", None),
        P("dp", "group", None),
        P(None, ("dp", "group"), None),
    )
    return jax.shard_map(
        on_device, mesh=mesh, in_specs=in_specs, out_specs=out_specs, check_vma=False
    )
```

```python
import functools

import jax
import jax.numpy as jnp
from jax import lax
from jax.experimental import pallas as pl
from jax.experimental.pallas import tpu as pltpu
from jax.sharding import PartitionSpec as P

delta_scale = 0.5
learn_rate = 0.005
beta_first = 0.9
beta_second = 0.999
adam_count = 20.0
adam_eps = 1e-08

BF = jnp.bfloat16
F32 = jnp.float32
MESH = pl.DeviceIdType.MESH

NZ, NX, NC = 4, 4, 2
NQ = NX * NC
NY, NH = 4, 2
D, FF, CAP, CAPD = 2048, 768, 20, 4
TOK, DEC = 128, 32
CHUNKS = ((0, 128), (128, 128)) + tuple((at, 256) for at in range(256, 2048, 256))
NCH = len(CHUNKS)
NP = 4
DCH = 4
CW = D // DCH
SB = NZ * CAP
DB = NZ * 2 * CAPD
PIECES = ((0, 512), (512, 768), (1280, 512), (1792, 1024))
W = D + FF


def nt(a, b):
    return lax.dot_general(a, b, (((1,), (1,)), ((), ())), preferred_element_type=F32)


def tn(a, b):
    return lax.dot_general(a, b, (((0,), (0,)), ((), ())), preferred_element_type=F32)


def mm(a, b):
    return jnp.dot(a, b, preferred_element_type=F32)


def iota(shape, axis):
    return lax.broadcasted_iota(jnp.int32, shape, axis)


def adam_update(parameter, moment_one, moment_two, gradient):
    first_new = beta_first * moment_one + (1.0 - beta_first) * gradient
    second_new = beta_second * moment_two + (1.0 - beta_second) * gradient * gradient
    fix_first = 1.0 - beta_first**adam_count
    fix_second = 1.0 - beta_second**adam_count
    update = first_new / fix_first / (jnp.sqrt(second_new / fix_second) + adam_eps)
    return (parameter - learn_rate * update, first_new, second_new)


def kernel(
    ids_ref, gates_ref, dids_ref, dgates_ref,
    fin_hbm, fout_hbm, cot_hbm, saved_hbm, base_hbm, min_hbm, mout_hbm, sin_hbm, sout_hbm, dh_hbm, res_hbm,
    hg_hbm, ain_hbm, vin_hbm, qin_hbm, aout_hbm, vout_hbm, qout_hbm, rout_hbm,
    fin_ref, fout_ref, ain_ref, vin_ref, qin_ref, aout_ref, vout_ref, qout_ref, rout_ref,
    xa, lms, lmr, dms, dmr, fg, pmat, lr, lg, ob, inc,
    saved, base, mi, mo, si, so, dh, res,
    perm, savedp, lit, lo, tg, ry, ss, sz, rz, rg,
    hgacc, hgp, hgn, dperm, dhp, dbase, amat, drs, pd, rd, pz, rzd,
    in_sem, out_sem, zt_s, zt_r, lm_s, lm_r, dm_s, dm_r, fz_s, fz_r, fy_s, fy_r,
    x_s, x_r, ry_s, ry_r, rz_s, rz_r, az_s, az_r, ay_s, ay_r, dx_s, dx_r, dz_s, dz_r,
):
    dp = lax.axis_index("dp")
    grp = lax.axis_index("group")
    z = dp // NQ
    q = dp % NQ
    x = q // NC
    c = q % NC
    y = grp // NH
    h = grp % NH

    def zdev(z2):
        return (z2 * NQ + q, grp)

    def qdev(q2):
        return (z * NQ + q2, grp)

    def ydev(y2):
        return (dp, y2 * NH + h)

    hdev = (dp, y * NH + (1 - h))
    zpeers = [(z + k) % NZ for k in (1, 2, 3)]
    ypeers = [(y + k) % NY for k in (2, 1, 3)]
    qpeers = [
        ((x + dx) % NX) * NC + (c + dc) % NC
        for dx, dc in ((2, 0), (2, 1), (1, 0), (3, 1), (1, 1), (3, 0), (0, 1))
    ]
    sends = []

    def push(src, dst, ssem, rsem, dev):
        cp = pltpu.make_async_remote_copy(
            src_ref=src, dst_ref=dst, send_sem=ssem, recv_sem=rsem, device_id=dev, device_id_type=MESH
        )
        cp.start()
        sends.append(cp)

    def arrived(dst, ssem, rsem, dev):
        pltpu.make_async_remote_copy(
            src_ref=dst, dst_ref=dst, send_sem=ssem, recv_sem=rsem, device_id=dev, device_id_type=MESH
        ).wait_recv()

    loads = {}

    def load(name, k, src, dst):
        cp = pltpu.make_async_copy(src, dst, in_sem.at[k])
        cp.start()
        loads[name] = cp

    def chunk(ch):
        return pl.ds(*CHUNKS[ch])

    own_rows = pl.ds(pl.multiple_of(z * TOK, TOK), TOK)
    for ch in range(NCH):
        load(("cot", ch), 10 + ch, cot_hbm.at[:, chunk(ch)], xa.at[own_rows, chunk(ch)])
    load("fin", 8, fin_hbm, fin_ref)
    load("fout", 9, fout_hbm, fout_ref)
    load("saved", 0, saved_hbm, saved)
    load("base", 1, base_hbm, base)
    load("dh", 2, dh_hbm, dh)
    load("mi", 3, min_hbm, mi)
    load("mo", 4, mout_hbm, mo)
    load("si", 5, sin_hbm, si)
    load("so", 6, sout_hbm, so)
    load("res", 7, res_hbm, res)

    barrier = pltpu.get_barrier_semaphore()
    for z2 in zpeers:
        pl.semaphore_signal(barrier, inc=1, device_id=zdev(z2), device_id_type=MESH)
    for q2 in qpeers:
        pl.semaphore_signal(barrier, inc=1, device_id=qdev(q2), device_id_type=MESH)
    for y2 in ypeers:
        pl.semaphore_signal(barrier, inc=1, device_id=ydev(y2), device_id_type=MESH)
    pl.semaphore_signal(barrier, inc=1, device_id=hdev, device_id_type=MESH)

    pl.semaphore_wait(barrier, 14)

    def send_tokens(ch):
        loads[("cot", ch)].wait()
        for k, z2 in enumerate(zpeers):
            part = xa.at[own_rows, chunk(ch)]
            push(part, part, zt_s.at[ch, k], zt_r.at[ch, z], zdev(z2))

    send_tokens(0)

    def tables(ids, gates):
        n = ids.shape[1]
        expert = iota((64, n), 0)
        count = jnp.zeros((64, n), F32)
        gate = jnp.zeros((64, n), F32)
        for k in range(8):
            hit = ids[k : k + 1, :] == expert
            count = count + jnp.where(hit, 1.0, 0.0)
            gate = gate + jnp.where(hit, gates[k : k + 1, :], 0.0)
        before = jnp.where(iota((n, n), 0) < iota((n, n), 1), 1.0, 0.0).astype(BF)
        return count > 0.5, mm(count.astype(BF), before), gate

    named, rank, gate = tables(ids_ref[...], gates_ref[...].astype(F32))
    row_t = jnp.where(named, rank + (CAP * z).astype(F32), -1.0).astype(BF)
    gate_t = gate.astype(BF)
    for z2 in range(NZ):
        lms[z2, 0:16] = row_t[16 * z2 : 16 * z2 + 16]
        lms[z2, 16:32] = gate_t[16 * z2 : 16 * z2 + 16]

    for k, z2 in enumerate(zpeers):
        push(lms.at[z2], lmr.at[z], lm_s.at[k], lm_r.at[z], zdev(z2))
    lmr[pl.ds(z, 1)] = lms[pl.ds(z, 1)]

    own = pl.ds(grp, 1)
    loads["fin"].wait()
    loads["fout"].wait()
    fg[own, :, 0:D] = fout_ref[...].astype(BF)[None]
    fg[own, :, D:W] = fin_ref[...].astype(BF)[None]

    push(fg.at[own], fg.at[own], fz_s.at[0], fz_r.at[0], hdev)

    flip = jnp.where(iota((64, 128), 0) == iota((64, 128), 1), 1.0, 0.0).astype(BF)
    for step in range(2):
        named, rank, gate = tables(dids_ref[step], dgates_ref[step])
        high = gate.astype(BF)
        low = (gate - high.astype(F32)).astype(BF)
        at = step * 16
        dms[at : at + 16] = tn(jnp.where(named, rank, -1.0).astype(BF), flip).astype(BF)
        dms[32 + at : 48 + at] = tn(high, flip).astype(BF)
        dms[64 + at : 80 + at] = tn(low, flip).astype(BF)

    for k, z2 in enumerate(zpeers):
        push(dms, dmr.at[z], dm_s.at[k], dm_r.at[z], zdev(z2))
    dmr[pl.ds(z, 1)] = dms[...][None]

    def permutation(source):
        n = source.shape[0]
        return jnp.where(iota((n, n), 1) == source, 1.0, 0.0).astype(BF)

    p_id = iota((NQ * SB, 1), 0)
    blk = (p_id * 3277) >> 16
    off = p_id - blk * CAP
    perm[0] = permutation((blk & 3) * (NQ * CAP) + (blk >> 2) * CAP + off)
    perm[1] = permutation((blk & 7) * SB + (blk >> 3) * CAP + off)

    for z2 in zpeers:
        arrived(lmr.at[z2], lm_s.at[0], lm_r.at[z2], zdev(z2))
    for z2 in range(NZ):
        lr[:, z2 * TOK : (z2 + 1) * TOK] = lmr[z2, 0:16].astype(F32)
        lg[:, z2 * TOK : (z2 + 1) * TOK] = lmr[z2, 16:32].astype(F32)
    slot = iota((SB, NZ * TOK), 0).astype(F32)

    def build_p(e, carry):
        row = lr[pl.ds(e, 1), :]
        val = lg[pl.ds(e, 1), :]
        pmat[e] = jnp.where(slot == row, val, 0.0).astype(BF)
        return carry

    lax.fori_loop(0, 2 * NQ, build_p, 0)

    def expand(ch, q2):
        w = pmat[pl.ds(q2 * 2, 2)].reshape(2 * SB, NZ * TOK)
        return mm(w, xa[:, chunk(ch)]).astype(BF).reshape(2, SB, CHUNKS[ch][1])

    def build_send(ch):
        for z2 in zpeers:
            dst = xa.at[pl.ds(pl.multiple_of(z2 * TOK, TOK), TOK), chunk(ch)]
            arrived(dst, zt_s.at[ch, 0], zt_r.at[ch, z2], zdev(z2))
        if ch == 0:
            send_tokens(1)
        if ch + 2 < NCH:
            send_tokens(ch + 2)
        cc = chunk(ch)
        for k, q2 in enumerate(qpeers):
            ob[k, :, :, cc] = expand(ch, q2)
            push(ob.at[k, :, :, cc], inc.at[:, q, :, cc], x_s.at[ch, k], x_r.at[ch, q], qdev(q2))
        inc[:, pl.ds(q, 1), :, cc] = expand(ch, q)[:, None]

    build_send(0)

    pair = pl.ds(pl.multiple_of(y * NH, NH), NH)
    other = pl.ds(y * NH + (1 - h), 1)
    arrived(fg.at[other], fz_s.at[0], fz_r.at[0], hdev)
    for k, y2 in enumerate(ypeers):
        push(fg.at[pair], fg.at[pair], fy_s.at[k], fy_r.at[y], ydev(y2))

    build_send(1)
    loads["saved"].wait()

    def permute_saved(e, carry):
        savedp[e] = mm(perm[0], saved[e]).astype(BF)
        return carry

    lax.fori_loop(0, 2, permute_saved, 0)
    build_send(2)

    for y2 in ypeers:
        blocks = pl.ds(pl.multiple_of(y2 * NH, NH), NH)
        arrived(fg.at[blocks], fy_s.at[0], fy_r.at[y2], ydev(y2))

    def lane_mask(n, e):
        return ((iota((n, 128), 1) >> 3) & 1) == e

    def low_in(e, carry):
        low = nt(savedp[e], fg[:, :, D:W].reshape(128, FF))
        low = jnp.where(lane_mask(NQ * SB, e), low, 0.0)
        lit[e] = low.T.astype(BF)
        lo[e] = jnp.zeros((NQ * SB, 128), F32)
        return carry

    lax.fori_loop(0, 2, low_in, 0)
    build_send(3)

    def consume(ch):
        for q2 in qpeers:
            arrived(inc.at[:, q2, :, chunk(ch)], x_s.at[ch, 0], x_r.at[ch, q2], qdev(q2))
        cc, cw = chunk(ch), CHUNKS[ch][1]
        weights = fg[:, :, cc].reshape(128, cw)

        def one(e, acc):
            rows = inc[e, :, :, cc].reshape(NQ * SB, cw)
            lo[e] += nt(rows, weights)
            return acc + mm(lit[e], rows)

        term = lax.fori_loop(0, 2, one, jnp.zeros((128, cw), F32))
        tg[:, :, cc] = term.astype(BF).reshape(8, 16, cw)

    def cols_of(p):
        return pl.ds(PIECES[p][0], PIECES[p][1])

    def rs_start(p):
        cc = cols_of(p)
        for k, y2 in enumerate(ypeers):
            src = tg.at[pl.ds(pl.multiple_of(y2 * NH, NH), NH), :, cc]
            push(src, ry.at[y, :, :, cc], ry_s.at[p, k], ry_r.at[p, y], ydev(y2))
        ry[pl.ds(y, 1), :, :, cc] = tg[pair, :, cc][None]

    def rs_mid(p):
        cc = cols_of(p)
        for y2 in ypeers:
            arrived(ry.at[y2, :, :, cc], ry_s.at[p, 0], ry_r.at[p, y2], ydev(y2))
        total = ry[0, :, :, cc].astype(F32)
        for y2 in range(1, NY):
            total = total + ry[y2, :, :, cc].astype(F32)
        ss[:, :, cc] = total
        sz[:, cc] = ss[1 - h, :, cc].astype(BF)
        push(sz.at[:, cc], rz.at[:, cc], rz_s.at[p], rz_r.at[p], hdev)

    def rs_fin(p):
        cc = cols_of(p)
        arrived(rz.at[:, cc], rz_s.at[p], rz_r.at[p], hdev)
        share = delta_scale / (NY * NH)

        def grad(start, width):
            at = pl.ds(start, width)
            return share * (ss[h, :, at] + rz[:, at].astype(F32))

        start = PIECES[p][0]
        width = min(PIECES[p][1], D - start)
        at = pl.ds(start, width)
        new, first, second = adam_update(fout_ref[:, at], mo[:, at], so[:, at], grad(start, width))
        aout_ref[:, at], vout_ref[:, at], qout_ref[:, at] = new, first, second
        rg[own, :, at] = new.astype(BF)[None]
        if p == NP - 1:
            new, first, second = adam_update(fin_ref[...], mi[...], si[...], grad(D, FF))
            ain_ref[...], vin_ref[...], qin_ref[...] = new, first, second
            rg[own, :, D:W] = new.astype(BF)[None]
        push(rg.at[own, :, cc], rg.at[own, :, cc], az_s.at[p], az_r.at[p], hdev)

    def ag_mid(p):
        cc = cols_of(p)
        arrived(rg.at[other, :, cc], az_s.at[p], az_r.at[p], hdev)
        for k, y2 in enumerate(ypeers):
            push(rg.at[pair, :, cc], rg.at[pair, :, cc], ay_s.at[p, k], ay_r.at[p, y], ydev(y2))

    def ag_fin(p):
        cc = cols_of(p)
        for y2 in ypeers:
            blocks = pl.ds(pl.multiple_of(y2 * NH, NH), NH)
            arrived(rg.at[blocks, :, cc], ay_s.at[p, 0], ay_r.at[p, y2], ydev(y2))

    consume(0)

    n = iota((512, 1), 0)
    source = ((n >> 2) & 1) * 256 + (n >> 8) * 128 + ((n >> 3) & 3) * 32 + ((n >> 5) & 7) * 4 + (n & 3)
    dperm[...] = permutation(source)
    loads["dh"].wait()
    dhp[...] = mm(dperm[...], dh[...]).astype(BF).reshape(2, 256, FF)

    build_send(4)
    consume(1)
    consume(2)
    rs_start(0)

    loads["base"].wait()

    def base_product(k, carry):
        e, ch = k // DCH, k % DCH
        at = pl.ds(pl.multiple_of(ch * CW, CW), CW)
        dbase[e, :, at] = mm(dhp[e], base[e, :, at])
        return carry

    lax.fori_loop(0, 2 * DCH, base_product, 0)
    build_send(5)
    consume(3)

    for z2 in zpeers:
        arrived(dmr.at[z2], dm_s.at[0], dm_r.at[z2], zdev(z2))
    for z2 in range(NZ):
        for k in range(3):
            drs[k, z2 * DEC : (z2 + 1) * DEC] = dmr[z2, k * DEC : (k + 1) * DEC]
    j = iota((128, 512), 1)
    spread = jnp.where(iota((128, 512), 0) == z * 16 + (j >> 5), 1.0, 0.0).astype(BF)
    i = iota((128, 512), 0)
    ok = (mm(drs[0], spread) == (j & 3).astype(F32)) & ((i >> 5) == ((j >> 3) & 3)) & (((i >> 4) & 1) == ((j >> 2) & 1))
    amat[0] = jnp.where(ok, mm(drs[1], spread), 0.0).astype(BF)
    amat[1] = jnp.where(ok, mm(drs[2], spread), 0.0).astype(BF)

    for name in ("mi", "mo", "si", "so", "res"):
        loads[name].wait()

    rs_mid(0)
    build_send(6)
    consume(4)
    build_send(7)
    consume(5)
    rs_start(1)
    rs_fin(0)
    build_send(8)
    consume(6)
    ag_mid(0)
    consume(7)
    rs_start(2)
    rs_mid(1)
    consume(8)

    def term_in(e, acc):
        low = jnp.where(lane_mask(NQ * SB, e), lo[e], 0.0)
        lo[e] = low
        return acc + mm(low.T.astype(BF), savedp[e])

    term = lax.fori_loop(0, 2, term_in, jnp.zeros((128, FF), F32))
    tg[:, :, D:W] = term.astype(BF).reshape(8, 16, FF)
    rs_start(3)
    rs_mid(2)
    rs_fin(1)

    def hidden(e):
        hgacc[...] = delta_scale * mm(lo[e].astype(BF), fg[:, :, D:W].reshape(128, FF))

        def part(ch, carry):
            at = pl.ds(pl.multiple_of(ch * CW, CW), CW)
            hgacc[...] += nt(inc[e, :, :, at].reshape(NQ * SB, CW), base[e, :, at])
            return carry

        lax.fori_loop(0, DCH, part, 0)
        hgp[...] = hgacc[...].astype(BF)
        hgn[e] = mm(perm[1], hgp[...]).astype(BF)
        cp = pltpu.make_async_copy(hgn.at[e], hg_hbm.at[e], out_sem.at[e])
        cp.start()
        return cp

    out0 = hidden(0)
    rs_mid(3)
    rs_fin(2)
    ag_mid(1)
    rs_fin(3)
    ag_mid(2)
    stores = []
    for k, (src, dst) in enumerate((
        (ain_ref, ain_hbm), (vin_ref, vin_hbm), (qin_ref, qin_hbm),
        (aout_ref, aout_hbm), (vout_ref, vout_hbm), (qout_ref, qout_hbm),
    )):
        stores.append(pltpu.make_async_copy(src, dst, out_sem.at[2 + k]))
        stores[-1].start()
    out1 = hidden(1)
    ag_mid(3)
    ag_fin(0)
    ag_fin(1)
    ag_fin(2)
    ag_fin(3)

    low_d = []
    for e in range(2):
        low = nt(dhp[e], rg[:, :, D:W].reshape(128, FF))
        low_d.append(jnp.where(lane_mask(256, e), low, 0.0).astype(BF))
    for ch in range(DCH):
        at = pl.ds(ch * CW, CW)
        weights = rg[:, :, at].reshape(128, CW)
        for e in range(2):
            made = dbase[e, :, at] + delta_scale * mm(low_d[e], weights)
            pd[ch, :, e] = made.astype(BF).reshape(NQ, DB, CW)
        for k, q2 in enumerate(qpeers):
            push(pd.at[ch, q2], rd.at[ch, q], dx_s.at[ch, k], dx_r.at[ch, q], qdev(q2))
        rd[ch, pl.ds(q, 1)] = pd[ch, pl.ds(q, 1)]
    for ch in range(DCH):
        for q2 in qpeers:
            arrived(rd.at[ch, q2], dx_s.at[ch, 0], dx_r.at[ch, q2], qdev(q2))
        rows = rd[ch].reshape(512, CW)
        part = mm(amat[0], rows) + mm(amat[1], rows)
        pz[ch] = part.astype(BF).reshape(NZ, DEC, CW)
        for k, z2 in enumerate(zpeers):
            push(pz.at[ch, z2], rzd.at[ch, z], dz_s.at[ch, k], dz_r.at[ch, z], zdev(z2))
        rzd[ch, pl.ds(z, 1)] = pz[ch, pl.ds(z, 1)]
    for ch in range(DCH):
        at = pl.ds(ch * CW, CW)
        for z2 in zpeers:
            arrived(rzd.at[ch, z2], dz_s.at[ch, 0], dz_r.at[ch, z2], zdev(z2))
        total = res[:, at].astype(F32)
        for z2 in range(NZ):
            total = total + rzd[ch, z2].astype(F32)
        rout_ref[:, at] = total.astype(BF)

    stores.append(pltpu.make_async_copy(rout_ref, rout_hbm, out_sem.at[8]))
    stores[-1].start()
    out0.wait()
    out1.wait()
    for cp in stores:
        cp.wait()
    for cp in sends:
        cp.wait_send()


def hand_over(*refs):
    made, results, held, sem = refs[:8], refs[8:16], refs[16:24], refs[24]
    arriving = [pltpu.make_async_copy(made[k], held[k], sem.at[0, k]) for k in range(8)]
    leaving = [pltpu.make_async_copy(held[k], results[k], sem.at[1, k]) for k in range(8)]
    for cp in arriving:
        cp.start()
    for k in (1, 2, 3, 4, 5, 6, 7, 0):
        arriving[k].wait()
        leaving[k].start()
    for cp in leaving:
        cp.wait()


def on_device(
    cotangent, gate_weights, expert_ids, saved_hidden, base_down, factor_in, factor_out,
    mean_in, mean_out, square_in, square_out, decode_hidden, decode_ids, decode_gates, residual_in,
):
    flat = lambda a: a.reshape(16, a.shape[-1])
    vm = pl.BlockSpec(memory_space=pltpu.VMEM)
    hbm = pl.BlockSpec(memory_space=pl.ANY)
    sds = jax.ShapeDtypeStruct
    V = pltpu.VMEM
    S = pltpu.SemaphoreType.DMA
    n = NQ * SB
    scratch = [
        V((16, FF), F32), V((16, D), F32),
        V((16, FF), F32), V((16, FF), F32), V((16, FF), F32),
        V((16, D), F32), V((16, D), F32), V((16, D), F32), V((DEC, D), BF),
        V((NZ * TOK, D), BF),
        V((NZ, 32, TOK), BF), V((NZ, 32, TOK), BF), V((96, 128), BF), V((NZ, 96, 128), BF),
        V((8, 16, W), BF),
        V((2 * NQ, SB, NZ * TOK), BF), V((16, NZ * TOK), F32), V((16, NZ * TOK), F32),
        V((7, 2, SB, D), BF), V((2, NQ, SB, D), BF),
        V((2, n, FF), BF), V((2, FF, D), BF),
        V((16, FF), F32), V((16, D), F32), V((16, FF), F32), V((16, D), F32),
        V((512, FF), BF), V((DEC, D), BF),
        V((2, n, n), BF), V((2, n, FF), BF), V((2, 128, n), BF), V((2, n, 128), F32),
        V((8, 16, W), BF), V((NY, NH, 16, W), BF), V((NH, 16, W), F32),
        V((16, W), BF), V((16, W), BF), V((8, 16, W), BF),
        V((n, FF), F32), V((n, FF), BF), V((2, n, FF), BF),
        V((512, 512), BF), V((2, 256, FF), BF), V((2, 256, D), F32),
        V((2, 128, 512), BF), V((3, 128, 128), BF),
        V((DCH, NQ, 2, DB, CW), BF), V((DCH, NQ, 2, DB, CW), BF),
        V((DCH, NZ, DEC, CW), BF), V((DCH, NZ, DEC, CW), BF),
        S((10 + NCH,)), S((9,)), S((NCH, 3)), S((NCH, NZ)), S((3,)), S((NZ,)), S((3,)), S((NZ,)),
        S((1,)), S((1,)), S((3,)), S((NY,)),
        S((NCH, 7)), S((NCH, NQ)), S((NP, 3)), S((NP, NY)), S((NP,)), S((NP,)),
        S((NP,)), S((NP,)), S((NP, 3)), S((NP, NY)),
        S((DCH, 7)), S((DCH, NQ)), S((DCH, 3)), S((DCH, NZ)),
    ]
    outs = pl.pallas_call(
        kernel,
        out_shape=(
            sds((2, n, FF), BF),
            sds((16, FF), F32), sds((16, FF), F32), sds((16, FF), F32),
            sds((16, D), F32), sds((16, D), F32), sds((16, D), F32),
            sds((DEC, D), BF),
        ),
        in_specs=[vm] * 4 + [hbm] * 11,
        out_specs=(hbm,) * 8,
        scratch_shapes=scratch,
        compiler_params=pltpu.CompilerParams(
            collective_id=0, has_side_effects=True, vmem_limit_bytes=60 * 1024 * 1024
        ),
    )(
        expert_ids.T, gate_weights.T, decode_ids.transpose(0, 2, 1), decode_gates.transpose(0, 2, 1),
        flat(factor_in), flat(factor_out),
        cotangent, saved_hidden, base_down, flat(mean_in), flat(mean_out), flat(square_in), flat(square_out),
        decode_hidden.reshape(512, FF), residual_in.reshape(DEC, D),
    )
    hg, ain, vin, qin, aout, vout, qout, rout = outs
    wide = lambda a: a.reshape(2, 8, a.shape[-1])
    made = (
        hg, wide(ain), wide(vin), wide(qin), wide(aout), wide(vout), wide(qout),
        rout.reshape(2, DEC // 2, D),
    )
    return pl.pallas_call(
        hand_over,
        out_shape=tuple(sds(a.shape, a.dtype) for a in made),
        in_specs=[hbm] * 8,
        out_specs=(hbm,) * 8,
        scratch_shapes=[V(a.shape, a.dtype) for a in made] + [S((2, 8))],
    )(*made)


def solution(mesh):
    in_specs = (
        P(("dp", "group"), None),
        P(("dp", "group"), None),
        P(("dp", "group"), None),
        P("dp", "group", None),
        P("dp", None, None),
        P("dp", "group", None),
        P("dp", "group", None),
        P("dp", "group", None),
        P("dp", "group", None),
        P("dp", "group", None),
        P("dp", "group", None),
        P(None, "dp", "group", None),
        P(None, ("dp", "group"), None),
        P(None, ("dp", "group"), None),
        P(None, ("dp", "group"), None),
    )
    out_specs = (
        P("dp", "group", None),
        P("dp", "group", None),
        P("dp", "group", None),
        P("dp", "group", None),
        P("dp", "group", None),
        P("dp", "group", None),
        P("dp", "group", None),
        P(None, ("dp", "group"), None),
    )
    return jax.shard_map(
        on_device, mesh=mesh, in_specs=in_specs, out_specs=out_specs, check_vma=False
    )
```

```python
import functools

import jax
import jax.numpy as jnp
from jax import lax
from jax.experimental import pallas as pl
from jax.experimental.pallas import tpu as pltpu
from jax.sharding import PartitionSpec as P

delta_scale = 0.5
learn_rate = 0.005
beta_first = 0.9
beta_second = 0.999
adam_count = 20.0
adam_eps = 1e-08

BF = jnp.bfloat16
F32 = jnp.float32
MESH = pl.DeviceIdType.MESH

NZ, NX, NC = 4, 4, 2
NQ = NX * NC
NY, NH = 4, 2
D, FF, CAP, CAPD = 2048, 768, 20, 4
TOK, DEC = 128, 32
CHUNKS = tuple((at, 256) for at in range(0, 2048, 256))
NCH = len(CHUNKS)
UNITS = (
    (0, 0), (1, 0), (0, 1), (1, 1), (0, 2), (0, 3), (1, 2), (0, 4), (0, 5), (1, 3), (0, 6), (0, 7),
    (1, 4), (1, 5), (1, 6), (1, 7),
)
LAG = 3
NP = 3
DCH = 4
CW = D // DCH
SB = NZ * CAP
DB = NZ * 2 * CAPD
PIECES = ((0, 1280), (1280, 512), (1792, 1024))
W = D + FF


def nt(a, b):
    return lax.dot_general(a, b, (((1,), (1,)), ((), ())), preferred_element_type=F32)


def tn(a, b):
    return lax.dot_general(a, b, (((0,), (0,)), ((), ())), preferred_element_type=F32)


def mm(a, b):
    return jnp.dot(a, b, preferred_element_type=F32)


def iota(shape, axis):
    return lax.broadcasted_iota(jnp.int32, shape, axis)


def adam_update(parameter, moment_one, moment_two, gradient):
    first_new = beta_first * moment_one + (1.0 - beta_first) * gradient
    second_new = beta_second * moment_two + (1.0 - beta_second) * gradient * gradient
    fix_first = 1.0 - beta_first**adam_count
    fix_second = 1.0 - beta_second**adam_count
    update = first_new / fix_first / (jnp.sqrt(second_new / fix_second) + adam_eps)
    return (parameter - learn_rate * update, first_new, second_new)


def kernel(
    ids_ref, gates_ref, dids_ref, dgates_ref,
    fin_hbm, fout_hbm, cot_hbm, saved_hbm, base_hbm, min_hbm, mout_hbm, sin_hbm, sout_hbm, dh_hbm, res_hbm,
    hg_hbm, ain_hbm, vin_hbm, qin_hbm, aout_hbm, vout_hbm, qout_hbm, rout_hbm,
    fin_ref, fout_ref, ain_ref, vin_ref, qin_ref, aout_ref, vout_ref, qout_ref, rout_ref,
    xa, lms, lmr, dms, dmr, fg, pmat, lr, lg, ob, inc,
    saved, base, mi, mo, si, so, dh, res,
    perm, savedp, lit, lo, tg, ry, ss, sz, rz, rh, ah, ar, rg,
    hgacc, hgp, hgn, dperm, dhp, dbase, amat, drs, pd, rd, pacc, pz, rzd,
    in_sem, out_sem, zt_s, zt_r, lm_s, lm_r, dm_s, dm_r, fz_s, fz_r, fy_s, fy_r,
    x_s, x_r, ry_s, ry_r, rz_s, rz_r, az_s, az_r, ay_s, ay_r, dx_s, dx_r, dz_s, dz_r,
):
    dp = lax.axis_index("dp")
    grp = lax.axis_index("group")
    z = dp // NQ
    q = dp % NQ
    x = q // NC
    c = q % NC
    y = grp // NH
    h = grp % NH

    def zdev(z2):
        return (z2 * NQ + q, grp)

    def qdev(q2):
        return (z * NQ + q2, grp)

    def ydev(y2):
        return (dp, y2 * NH + h)

    hdev = (dp, y * NH + (1 - h))
    zpeers = [(z + k) % NZ for k in (1, 2, 3)]
    ypeers = [(y + k) % NY for k in (2, 1, 3)]
    qpeers = [
        ((x + dx) % NX) * NC + (c + dc) % NC
        for dx, dc in ((2, 0), (2, 1), (1, 0), (3, 1), (1, 1), (3, 0), (0, 1))
    ]
    barrier = pltpu.get_barrier_semaphore()
    for z2 in zpeers:
        pl.semaphore_signal(barrier, inc=1, device_id=zdev(z2), device_id_type=MESH)
    for q2 in qpeers:
        pl.semaphore_signal(barrier, inc=1, device_id=qdev(q2), device_id_type=MESH)
    for y2 in ypeers:
        pl.semaphore_signal(barrier, inc=1, device_id=ydev(y2), device_id_type=MESH)
    pl.semaphore_signal(barrier, inc=1, device_id=hdev, device_id_type=MESH)

    sends = []

    def push(src, dst, ssem, rsem, dev):
        cp = pltpu.make_async_remote_copy(
            src_ref=src, dst_ref=dst, send_sem=ssem, recv_sem=rsem, device_id=dev, device_id_type=MESH
        )
        cp.start()
        sends.append(cp)

    def arrived(dst, ssem, rsem, dev):
        pltpu.make_async_remote_copy(
            src_ref=dst, dst_ref=dst, send_sem=ssem, recv_sem=rsem, device_id=dev, device_id_type=MESH
        ).wait_recv()

    loads = {}

    def load(name, k, src, dst):
        cp = pltpu.make_async_copy(src, dst, in_sem.at[k])
        cp.start()
        loads[name] = cp

    def chunk(ch):
        return pl.ds(*CHUNKS[ch])

    own_rows = pl.ds(pl.multiple_of(z * TOK, TOK), TOK)
    for ch in range(NCH):
        load(("cot", ch), 10 + ch, cot_hbm.at[:, chunk(ch)], xa.at[own_rows, chunk(ch)])
    load("fin", 8, fin_hbm, fin_ref)
    load("fout", 9, fout_hbm, fout_ref)
    load("saved", 0, saved_hbm, saved)
    load("base", 1, base_hbm, base)
    load("dh", 2, dh_hbm, dh)
    load("mi", 3, min_hbm, mi)
    load("mo", 4, mout_hbm, mo)
    load("si", 5, sin_hbm, si)
    load("so", 6, sout_hbm, so)
    load("res", 7, res_hbm, res)

    def tables(ids, gates):
        n = ids.shape[1]
        expert = iota((64, n), 0)
        count = jnp.zeros((64, n), F32)
        gate = jnp.zeros((64, n), F32)
        for k in range(8):
            hit = ids[k : k + 1, :] == expert
            count = count + jnp.where(hit, 1.0, 0.0)
            gate = gate + jnp.where(hit, gates[k : k + 1, :], 0.0)
        before = jnp.where(iota((n, n), 0) < iota((n, n), 1), 1.0, 0.0).astype(BF)
        return count > 0.5, mm(count.astype(BF), before), gate

    named, rank, gate = tables(ids_ref[...], gates_ref[...].astype(F32))
    row_t = jnp.where(named, rank + (CAP * z).astype(F32), -1.0).astype(BF)
    gate_t = gate.astype(BF)
    for z2 in range(NZ):
        lms[z2, 0:16] = row_t[16 * z2 : 16 * z2 + 16]
        lms[z2, 16:32] = gate_t[16 * z2 : 16 * z2 + 16]

    pl.semaphore_wait(barrier, 14)

    leaving = []
    left = set()

    def send_tokens(ch):
        loads[("cot", ch)].wait()
        for k, z2 in enumerate(zpeers):
            part = xa.at[own_rows, chunk(ch)]
            leaving.append((ch, len(sends)))
            push(part, part, zt_s.at[ch, k], zt_r.at[ch, z], zdev(z2))

    send_tokens(0)
    for k, z2 in enumerate(zpeers):
        push(lms.at[z2], lmr.at[z], lm_s.at[k], lm_r.at[z], zdev(z2))
    lmr[pl.ds(z, 1)] = lms[pl.ds(z, 1)]

    own = pl.ds(grp, 1)
    loads["fin"].wait()
    loads["fout"].wait()
    fg[own, :, 0:D] = fout_ref[...].astype(BF)[None]
    fg[own, :, D:W] = fin_ref[...].astype(BF)[None]

    push(fg.at[own], fg.at[own], fz_s.at[0], fz_r.at[0], hdev)

    flip = jnp.where(iota((64, 128), 0) == iota((64, 128), 1), 1.0, 0.0).astype(BF)
    for step in range(2):
        named, rank, gate = tables(dids_ref[step], dgates_ref[step])
        high = gate.astype(BF)
        low = (gate - high.astype(F32)).astype(BF)
        at = step * 16
        dms[at : at + 16] = tn(jnp.where(named, rank, -1.0).astype(BF), flip).astype(BF)
        dms[32 + at : 48 + at] = tn(high, flip).astype(BF)
        dms[64 + at : 80 + at] = tn(low, flip).astype(BF)

    for k, z2 in enumerate(zpeers):
        push(dms, dmr.at[z], dm_s.at[k], dm_r.at[z], zdev(z2))
    dmr[pl.ds(z, 1)] = dms[...][None]

    def permutation(source):
        n = source.shape[0]
        return jnp.where(iota((n, n), 1) == source, 1.0, 0.0).astype(BF)

    p_id = iota((NQ * SB, 1), 0)
    blk = (p_id * 3277) >> 16
    off = p_id - blk * CAP
    perm[0] = permutation((blk & 3) * (NQ * CAP) + (blk >> 2) * CAP + off)
    perm[1] = permutation((blk & 7) * SB + (blk >> 3) * CAP + off)

    for z2 in zpeers:
        arrived(lmr.at[z2], lm_s.at[0], lm_r.at[z2], zdev(z2))
    for z2 in range(NZ):
        lr[:, z2 * TOK : (z2 + 1) * TOK] = lmr[z2, 0:16].astype(F32)
        lg[:, z2 * TOK : (z2 + 1) * TOK] = lmr[z2, 16:32].astype(F32)
    slot = iota((SB, NZ * TOK), 0).astype(F32)

    for e in range(2):

        def build_p(q2, carry):
            row = lr[pl.ds(q2 * 2 + e, 1), :]
            val = lg[pl.ds(q2 * 2 + e, 1), :]
            pmat[e, q2] = jnp.where(slot == row, val, 0.0).astype(BF)
            return carry

        lax.fori_loop(0, NQ, build_p, 0)

    def tokens(ch):
        for of, k in leaving:
            if of == ch:
                sends[k].wait_send()
                left.add(k)
        if ch + 1 < NCH:
            send_tokens(ch + 1)
        for z2 in zpeers:
            dst = xa.at[pl.ds(pl.multiple_of(z2 * TOK, TOK), TOK), chunk(ch)]
            arrived(dst, zt_s.at[ch, 0], zt_r.at[ch, z2], zdev(z2))

    def build_send(e, ch):
        cc, at = chunk(ch), e * NCH + ch
        made = mm(pmat[e].reshape(NQ * SB, NZ * TOK), xa[:, cc])
        ob[e, :, :, cc] = made.astype(BF).reshape(NQ, SB, CHUNKS[ch][1])
        for k, q2 in enumerate(qpeers):
            push(ob.at[e, q2, :, cc], inc.at[e, q, :, cc], x_s.at[at, k], x_r.at[at, q], qdev(q2))
        inc[e, pl.ds(q, 1), :, cc] = ob[e, pl.ds(q, 1), :, cc]

    def lane_mask(n, e):
        return ((iota((n, 128), 1) >> 3) & 1) == e

    def own_ranks(low, e):
        n = low.shape[0]
        return low.T.reshape(8, 2, 8, n)[:, e].reshape(64, n).astype(BF)

    def consume(e, ch):
        cc, cw, at = chunk(ch), CHUNKS[ch][1], e * NCH + ch
        for q2 in qpeers:
            arrived(inc.at[e, q2, :, cc], x_s.at[at, 0], x_r.at[at, q2], qdev(q2))
        rows = inc[e, :, :, cc].reshape(NQ * SB, cw)
        lo[e] += nt(rows, fg[:, :, cc].reshape(128, cw))
        tg[e, :, :, cc] = mm(lit[e], rows).astype(BF).reshape(NY, 16, cw)

    def term_in(e):
        low = jnp.where(lane_mask(NQ * SB, e), lo[e], 0.0)
        lo[e] = low
        tg[e, :, :, D:W] = mm(own_ranks(low, e), savedp[e]).astype(BF).reshape(NY, 16, FF)

    def cols_of(p):
        return pl.ds(PIECES[p][0], PIECES[p][1])

    def half(p):
        return pl.ds(PIECES[p][0] // 2, PIECES[p][1] // 2)

    def pack(a):
        n = a.shape[1] // 2
        return jnp.concatenate([a[:, :n], a[:, n:]], axis=0).astype(BF)

    def unpack(a):
        a = a.astype(F32)
        return jnp.concatenate([a[:8], a[8:]], axis=1)

    def rs_start(e, p):
        cc, at = cols_of(p), e * NP + p
        for k, y2 in enumerate(ypeers):
            push(tg.at[e, y2, :, cc], ry.at[e, y, :, cc], ry_s.at[at, k], ry_r.at[at, y], ydev(y2))
        ry[e, pl.ds(y, 1), :, cc] = tg[e, pl.ds(y, 1), :, cc]

    def rs_mid(e, p):
        cc, at = cols_of(p), e * NP + p
        for y2 in ypeers:
            arrived(ry.at[e, y2, :, cc], ry_s.at[at, 0], ry_r.at[at, y2], ydev(y2))
        total = ry[e, 0, :, cc].astype(F32)
        for y2 in range(1, NY):
            total = total + ry[e, y2, :, cc].astype(F32)
        ss[e, :, :, cc] = total.reshape(NH, 8, PIECES[p][1])
        sz[e, :, half(p)] = pack(ss[e, pl.ds(1 - h, 1), :, cc].reshape(8, PIECES[p][1]))
        push(sz.at[e, :, half(p)], rz.at[e, :, half(p)], rz_s.at[at], rz_r.at[at], hdev)

    def rs_fin(e, p):
        cc, at = cols_of(p), e * NP + p
        arrived(rz.at[e, :, half(p)], rz_s.at[at], rz_r.at[at], hdev)
        share = delta_scale / (NY * NH)
        er = pl.ds(e * 8, 8)
        start, width = PIECES[p]
        own_sum = ss[e, pl.ds(h, 1), :, cc].reshape(8, width)
        grad = share * (own_sum + unpack(rz[e, :, half(p)]))
        n = min(width, D - start)
        part = pl.ds(start, n)
        new, first, second = adam_update(fout_ref[er, part], mo[er, part], so[er, part], grad[:, :n])
        aout_ref[er, part], vout_ref[er, part], qout_ref[er, part] = new, first, second
        if p == NP - 1:
            new_in, first, second = adam_update(fin_ref[er, :], mi[er, :], si[er, :], grad[:, n:])
            ain_ref[er, :], vin_ref[er, :], qin_ref[er, :] = new_in, first, second
            new = jnp.concatenate([new, new_in], axis=1)
        rh[e, pl.ds(h, 1), :, cc] = new[None]
        ah[e, :, half(p)] = pack(new)
        push(ah.at[e, :, half(p)], ar.at[e, :, half(p)], az_s.at[at], az_r.at[at], hdev)

    def ag_mid(e, p):
        cc, at = cols_of(p), e * NP + p
        arrived(ar.at[e, :, half(p)], az_s.at[at], az_r.at[at], hdev)
        rh[e, pl.ds(1 - h, 1), :, cc] = unpack(ar[e, :, half(p)])[None]
        rg[e, pl.ds(y, 1), :, cc] = rh[e, :, :, cc].reshape(1, 16, PIECES[p][1]).astype(BF)
        for k, y2 in enumerate(ypeers):
            push(rg.at[e, y, :, cc], rg.at[e, y, :, cc], ay_s.at[at, k], ay_r.at[at, y], ydev(y2))

    def ag_fin(e, p):
        cc, at = cols_of(p), e * NP + p
        for y2 in ypeers:
            arrived(rg.at[e, y2, :, cc], ay_s.at[at, 0], ay_r.at[at, y2], ydev(y2))

    def hidden(e):
        hgacc[...] = delta_scale * mm(lo[e].astype(BF), fg[:, :, D:W].reshape(128, FF))

        def part(ch, carry):
            at = pl.ds(pl.multiple_of(ch * CW, CW), CW)
            hgacc[...] += nt(inc[e, :, :, at].reshape(NQ * SB, CW), base[e, :, at])
            return carry

        lax.fori_loop(0, DCH, part, 0)
        hgp[...] = hgacc[...].astype(BF)
        hgn[e] = mm(perm[1], hgp[...]).astype(BF)
        cp = pltpu.make_async_copy(hgn.at[e], hg_hbm.at[e], out_sem.at[e])
        cp.start()
        return cp

    def decode_send(e):
        low = nt(dhp[e], rg[e, :, :, D:W].reshape(64, FF)).astype(BF)
        for ch in range(DCH):
            part, at = pl.ds(ch * CW, CW), e * DCH + ch
            made = dbase[e, :, part] + delta_scale * mm(low, rg[e, :, :, part].reshape(64, CW))
            pd[e, ch] = made.astype(BF).reshape(NQ, DB, CW)
            for k, q2 in enumerate(qpeers):
                push(pd.at[e, ch, q2], rd.at[e, ch, q], dx_s.at[at, k], dx_r.at[at, q], qdev(q2))
            rd[e, ch, pl.ds(q, 1)] = pd[e, ch, pl.ds(q, 1)]

    def gated(e, ch):
        at = e * DCH + ch
        for q2 in qpeers:
            arrived(rd.at[e, ch, q2], dx_s.at[at, 0], dx_r.at[at, q2], qdev(q2))
        rows = rd[e, ch].reshape(256, CW)
        return mm(amat[0, :, e * 256 : e * 256 + 256], rows) + mm(amat[1, :, e * 256 : e * 256 + 256], rows)

    def share_factors():
        pair = pl.ds(pl.multiple_of(y * NH, NH), NH)
        other = pl.ds(y * NH + (1 - h), 1)
        arrived(fg.at[other], fz_s.at[0], fz_r.at[0], hdev)
        for k, y2 in enumerate(ypeers):
            push(fg.at[pair], fg.at[pair], fy_s.at[k], fy_r.at[y], ydev(y2))

    def order_saved():
        loads["saved"].wait()

        def permute_saved(e, carry):
            savedp[e] = mm(perm[0], saved[e]).astype(BF)
            return carry

        lax.fori_loop(0, 2, permute_saved, 0)

    def low_inputs():
        for y2 in ypeers:
            blocks = pl.ds(pl.multiple_of(y2 * NH, NH), NH)
            arrived(fg.at[blocks], fy_s.at[0], fy_r.at[y2], ydev(y2))

        for e in range(2):
            lit[e] = own_ranks(nt(savedp[e], fg[:, :, D:W].reshape(128, FF)), e)
            lo[e] = jnp.zeros((NQ * SB, 128), F32)

    def order_decode():
        n = iota((512, 1), 0)
        source = ((n >> 2) & 1) * 256 + (n >> 8) * 128 + ((n >> 3) & 3) * 32 + ((n >> 5) & 7) * 4 + (n & 3)
        dperm[...] = permutation(source)
        loads["dh"].wait()
        dhp[...] = mm(dperm[...], dh[...]).astype(BF).reshape(2, 256, FF)

    def gate_matrix():
        for z2 in zpeers:
            arrived(dmr.at[z2], dm_s.at[0], dm_r.at[z2], zdev(z2))
        for z2 in range(NZ):
            for k in range(3):
                drs[k, z2 * DEC : (z2 + 1) * DEC] = dmr[z2, k * DEC : (k + 1) * DEC]
        j = iota((128, 512), 1)
        spread = jnp.where(iota((128, 512), 0) == z * 16 + ((j >> 5) & 7) * 2 + (j >> 8), 1.0, 0.0).astype(BF)
        i = iota((128, 512), 0)
        ok = (mm(drs[0], spread) == (j & 3).astype(F32)) & ((i >> 5) == ((j >> 3) & 3)) & (((i >> 4) & 1) == ((j >> 2) & 1))
        amat[0] = jnp.where(ok, mm(drs[1], spread), 0.0).astype(BF)
        amat[1] = jnp.where(ok, mm(drs[2], spread), 0.0).astype(BF)

        for name in ("mi", "mo", "si", "so", "res"):
            loads[name].wait()

    def base_products():
        loads["base"].wait()

        def base_product(k, carry):
            e, ch = k // DCH, k % DCH
            at = pl.ds(pl.multiple_of(ch * CW, CW), CW)
            dbase[e, :, at] = mm(dhp[e], base[e, :, at])
            return carry

        lax.fori_loop(0, 2 * DCH, base_product, 0)

    done_with = {}

    def hide():
        done_with["out0"] = hidden(0)

    before = {
        1: [share_factors], 3: [order_saved], 5: [low_inputs], 6: [order_decode], 8: [gate_matrix], 9: [base_products],
    }
    after = {
        7: [(rs_start, 0, 0)],
        9: [(rs_mid, 0, 0)],
        10: [(rs_start, 0, 1), (rs_fin, 0, 0)],
        11: [(term_in, 0), (rs_start, 0, 2), (rs_mid, 0, 1), (ag_mid, 0, 0)],
        12: [(rs_start, 1, 0), (rs_mid, 0, 2), (rs_fin, 0, 1), (hide,)],
        13: [(rs_fin, 0, 2), (ag_mid, 0, 1), (rs_mid, 1, 0)],
        14: [(rs_start, 1, 1), (ag_mid, 0, 2), (rs_fin, 1, 0)],
        15: [(term_in, 1), (rs_start, 1, 2), (rs_mid, 1, 1), (ag_mid, 1, 0)],
    }
    used = 0
    for k, (e, ch) in enumerate(UNITS):
        for task in before.get(k, ()):
            task()
        if e == 0:
            tokens(ch)
        build_send(e, ch)
        while k >= 5 and used <= k - LAG or k == len(UNITS) - 1 and used < len(UNITS):
            consume(*UNITS[used])
            for task in after.get(used, ()):
                task[0](*task[1:])
            used += 1

    for p in range(NP):
        ag_fin(0, p)
    decode_send(0)
    rs_mid(1, 2)
    rs_fin(1, 1)
    rs_fin(1, 2)
    ag_mid(1, 1)
    stores = []
    for k, (src, dst) in enumerate((
        (ain_ref, ain_hbm), (vin_ref, vin_hbm), (qin_ref, qin_hbm),
        (aout_ref, aout_hbm), (vout_ref, vout_hbm), (qout_ref, qout_hbm),
    )):
        stores.append(pltpu.make_async_copy(src, dst, out_sem.at[2 + k]))
        stores[-1].start()
    ag_mid(1, 2)
    for p in range(NP):
        ag_fin(1, p)
    decode_send(1)
    for ch in range(DCH):
        pacc[ch] = gated(0, ch)
    out0 = done_with["out0"]
    out1 = hidden(1)

    for ch in range(DCH):
        part = pacc[ch] + gated(1, ch)
        pz[ch] = part.astype(BF).reshape(NZ, DEC, CW)
        for k, z2 in enumerate(zpeers):
            push(pz.at[ch, z2], rzd.at[ch, z], dz_s.at[ch, k], dz_r.at[ch, z], zdev(z2))
        rzd[ch, pl.ds(z, 1)] = pz[ch, pl.ds(z, 1)]
    for ch in range(DCH):
        at = pl.ds(ch * CW, CW)
        for z2 in zpeers:
            arrived(rzd.at[ch, z2], dz_s.at[ch, 0], dz_r.at[ch, z2], zdev(z2))
        total = res[:, at].astype(F32)
        for z2 in range(NZ):
            total = total + rzd[ch, z2].astype(F32)
        rout_ref[:, at] = total.astype(BF)

    stores.append(pltpu.make_async_copy(rout_ref, rout_hbm, out_sem.at[8]))
    stores[-1].start()
    out0.wait()
    out1.wait()
    for cp in stores:
        cp.wait()
    for k, cp in enumerate(sends):
        if k not in left:
            cp.wait_send()


def hand_over(*refs):
    made, results, held, sem = refs[:8], refs[8:16], refs[16:24], refs[24]
    arriving = [pltpu.make_async_copy(made[k], held[k], sem.at[0, k]) for k in range(8)]
    leaving = [pltpu.make_async_copy(held[k], results[k], sem.at[1, k]) for k in range(8)]
    for cp in arriving:
        cp.start()
    for k in (1, 2, 3, 4, 5, 6, 7, 0):
        arriving[k].wait()
        leaving[k].start()
    for cp in leaving:
        cp.wait()


def on_device(
    cotangent, gate_weights, expert_ids, saved_hidden, base_down, factor_in, factor_out,
    mean_in, mean_out, square_in, square_out, decode_hidden, decode_ids, decode_gates, residual_in,
):
    flat = lambda a: a.reshape(16, a.shape[-1])
    vm = pl.BlockSpec(memory_space=pltpu.VMEM)
    hbm = pl.BlockSpec(memory_space=pl.ANY)
    sds = jax.ShapeDtypeStruct
    V = pltpu.VMEM
    S = pltpu.SemaphoreType.DMA
    n = NQ * SB
    scratch = [
        V((16, FF), F32), V((16, D), F32),
        V((16, FF), F32), V((16, FF), F32), V((16, FF), F32),
        V((16, D), F32), V((16, D), F32), V((16, D), F32), V((DEC, D), BF),
        V((NZ * TOK, D), BF),
        V((NZ, 32, TOK), BF), V((NZ, 32, TOK), BF), V((96, 128), BF), V((NZ, 96, 128), BF),
        V((8, 16, W), BF),
        V((2, NQ, SB, NZ * TOK), BF), V((16, NZ * TOK), F32), V((16, NZ * TOK), F32),
        V((2, NQ, SB, D), BF), V((2, NQ, SB, D), BF),
        V((2, n, FF), BF), V((2, FF, D), BF),
        V((16, FF), F32), V((16, D), F32), V((16, FF), F32), V((16, D), F32),
        V((512, FF), BF), V((DEC, D), BF),
        V((2, n, n), BF), V((2, n, FF), BF), V((2, 64, n), BF), V((2, n, 128), F32),
        V((2, NY, 16, W), BF), V((2, NY, 16, W), BF), V((2, NH, 8, W), F32),
        V((2, 16, W // 2), BF), V((2, 16, W // 2), BF), V((2, NH, 8, W), F32),
        V((2, 16, W // 2), BF), V((2, 16, W // 2), BF), V((2, NY, 16, W), BF),
        V((n, FF), F32), V((n, FF), BF), V((2, n, FF), BF),
        V((512, 512), BF), V((2, 256, FF), BF), V((2, 256, D), F32),
        V((2, 128, 512), BF), V((3, 128, 128), BF),
        V((2, DCH, NQ, DB, CW), BF), V((2, DCH, NQ, DB, CW), BF), V((DCH, 128, CW), F32),
        V((DCH, NZ, DEC, CW), BF), V((DCH, NZ, DEC, CW), BF),
        S((10 + NCH,)), S((9,)), S((NCH, 3)), S((NCH, NZ)), S((3,)), S((NZ,)), S((3,)), S((NZ,)),
        S((1,)), S((1,)), S((3,)), S((NY,)),
        S((2 * NCH, 7)), S((2 * NCH, NQ)), S((2 * NP, 3)), S((2 * NP, NY)), S((2 * NP,)), S((2 * NP,)),
        S((2 * NP,)), S((2 * NP,)), S((2 * NP, 3)), S((2 * NP, NY)),
        S((2 * DCH, 7)), S((2 * DCH, NQ)), S((DCH, 3)), S((DCH, NZ)),
    ]
    outs = pl.pallas_call(
        kernel,
        out_shape=(
            sds((2, n, FF), BF),
            sds((16, FF), F32), sds((16, FF), F32), sds((16, FF), F32),
            sds((16, D), F32), sds((16, D), F32), sds((16, D), F32),
            sds((DEC, D), BF),
        ),
        in_specs=[vm] * 4 + [hbm] * 11,
        out_specs=(hbm,) * 8,
        scratch_shapes=scratch,
        compiler_params=pltpu.CompilerParams(
            collective_id=0, has_side_effects=True, vmem_limit_bytes=60 * 1024 * 1024
        ),
    )(
        expert_ids.T, gate_weights.T, decode_ids.transpose(0, 2, 1), decode_gates.transpose(0, 2, 1),
        flat(factor_in), flat(factor_out),
        cotangent, saved_hidden, base_down, flat(mean_in), flat(mean_out), flat(square_in), flat(square_out),
        decode_hidden.reshape(512, FF), residual_in.reshape(DEC, D),
    )
    hg, ain, vin, qin, aout, vout, qout, rout = outs
    wide = lambda a: a.reshape(2, 8, a.shape[-1])
    made = (
        hg, wide(ain), wide(vin), wide(qin), wide(aout), wide(vout), wide(qout),
        rout.reshape(2, DEC // 2, D),
    )
    return pl.pallas_call(
        hand_over,
        out_shape=tuple(sds(a.shape, a.dtype) for a in made),
        in_specs=[hbm] * 8,
        out_specs=(hbm,) * 8,
        scratch_shapes=[V(a.shape, a.dtype) for a in made] + [S((2, 8))],
    )(*made)


def solution(mesh):
    in_specs = (
        P(("dp", "group"), None),
        P(("dp", "group"), None),
        P(("dp", "group"), None),
        P("dp", "group", None),
        P("dp", None, None),
        P("dp", "group", None),
        P("dp", "group", None),
        P("dp", "group", None),
        P("dp", "group", None),
        P("dp", "group", None),
        P("dp", "group", None),
        P(None, "dp", "group", None),
        P(None, ("dp", "group"), None),
        P(None, ("dp", "group"), None),
        P(None, ("dp", "group"), None),
    )
    out_specs = (
        P("dp", "group", None),
        P("dp", "group", None),
        P("dp", "group", None),
        P("dp", "group", None),
        P("dp", "group", None),
        P("dp", "group", None),
        P("dp", "group", None),
        P(None, ("dp", "group"), None),
    )
    return jax.shard_map(
        on_device, mesh=mesh, in_specs=in_specs, out_specs=out_specs, check_vma=False
    )
```
